512 devices in a mesh: seq: 128 (over z, x, core), head: 4 (over y).
Axes of the slice: x: 4, y: 4, z: 16, core: 2. Of those that a mesh axis runs over, the one named last changes fastest.
Arguments:
- queries: bfloat16 [65536, 2048], P('seq', 'head'), may hold values from -6 to 6
- keys: bfloat16 [65536, 2048], P('seq', 'head'), may hold values from -6 to 6
- values: bfloat16 [65536, 2048], P('seq', 'head'), may hold values from -6 to 6
- grad_out: bfloat16 [65536, 2048], P('seq', 'head'), may hold values from -24 to 24
- out_weight: bfloat16 [2048, 2048], P('seq', 'head'), may hold values from -0.125 to 0.125
Outputs:
- query_grad: bfloat16 [65536, 2048], P('seq', 'head')
- key_grad: bfloat16 [65536, 2048], P('seq', 'head')
- value_grad: bfloat16 [65536, 2048], P('seq', 'head')
- weight_grad: float32 [2048, 2048], P('seq', 'head')
The draws below stay inside these ranges and needn't reach their ends.
All inputs are finite; a program needn't handle non-finite values.
Results may differ from the reference program's by a relative error of at most 0.0057.
Values may be sent and summed in bfloat16 or wider, within the bound.
A program may use at most 192 MiB of HBM per device.

```python
import math
import jax
import jax.numpy as jnp
from jax import lax

HEADS = 16
HEAD_DIM = 128
DOUT = 2048
TOK_DEV = 512
TOKENS = 65536


def strengthened(entries, rng, source, target, parts, factor):
    owner, partner = [(jnp.arange(entries.shape[axis_at]) // (entries.shape[axis_at] // parts)).reshape([-1 if axis == axis_at else 1 for axis in range(entries.ndim)]) for axis_at in (source, target)]
    chosen = jax.random.permutation(rng, parts)[partner]
    strong = (owner == chosen) | (owner == (partner + parts // 2) % parts)
    return jnp.where(strong, factor * entries, entries)


def levels(rng, shape, pieces, low, high):
    factor_of, own = 1.0, jax.random.fold_in(rng, 6)
    for dim, parts in pieces:
        steps = jnp.exp(jax.random.uniform(jax.random.fold_in(own, dim), (parts,), jnp.float32, low / len(pieces), high / len(pieces)))
        factor_of = factor_of * jnp.repeat(steps, shape[dim] // parts).reshape([-1 if axis == dim else 1 for axis in range(len(shape))])
    return factor_of


def scatter_about(own_key, extent, scale, reach, pieces=(), kind=jnp.bfloat16):
    factor_of = levels(own_key, extent, pieces, -0.22, 0.18) if pieces else 1.0
    entries = jax.random.normal(own_key, extent, jnp.float32) * scale * factor_of
    return jnp.minimum(jnp.maximum(entries, -reach), reach).astype(kind)


def noise_with(rng, extent, scale, limit, cuts, heavy, dtype=jnp.bfloat16):
    array = scale * jax.random.normal(rng, extent, jnp.float32)
    if cuts:
        array = array * levels(rng, extent, cuts, -0.22, 0.18)
    return jnp.clip(strengthened(array, jax.random.fold_in(rng, 3), *heavy), -limit, limit).astype(dtype)


def setup_inputs(seed: int = 0) -> dict:
    streams_of = jax.random.split(jax.random.key(seed), 6)
    queries = scatter_about(streams_of[0], (TOKENS, HEADS * HEAD_DIM), 1.0, 6.0, ((0, 128), (1, 4)))
    keys = scatter_about(streams_of[1], (TOKENS, HEADS * HEAD_DIM), 1.0, 6.0, ((0, 128), (1, 4)))
    values = scatter_about(streams_of[2], (TOKENS, HEADS * HEAD_DIM), 1.0, 6.0, ((0, 128), (1, 4)))
    grad_out = noise_with(streams_of[3], (TOKENS, DOUT), 1.0, 24.0, ((0, 128), (1, 4)), (0, 1, 128, 5.5))
    out_weight = scatter_about(streams_of[4], (DOUT, HEADS * HEAD_DIM), DOUT ** -0.5, 0.125, ((0, 128), (1, 4)))
    return dict(queries=queries, keys=keys, values=values, grad_out=grad_out, out_weight=out_weight)


def reference(queries, keys, values, grad_out, out_weight):
    scale = 1.0 / math.sqrt(HEAD_DIM * TOKENS)
    attn_grad = jnp.dot(grad_out, out_weight, preferred_element_type=jnp.float32).astype(jnp.bfloat16)
    blocks = TOKENS // TOK_DEV

    def split(arr):
        return arr.reshape(blocks, TOK_DEV, HEADS, HEAD_DIM)
    q_all, k_all, v_all, g_all = (split(queries), split(keys), split(values), split(attn_grad))

    def block_states(items):
        q_blk, k_blk, v_blk, g_blk = items
        kv_blk = jnp.einsum('thi,thj->hij', k_blk.astype(jnp.float32), v_blk.astype(jnp.float32))
        qg_blk = jnp.einsum('thi,thj->hij', q_blk.astype(jnp.float32), g_blk.astype(jnp.float32))
        return (kv_blk, qg_blk)
    kv_all, qg_all = lax.map(block_states, (q_all, k_all, v_all, g_all))
    prefix_all = (jnp.cumsum(kv_all, axis=0) - kv_all).astype(jnp.bfloat16)
    suffix_all = (jnp.flip(jnp.cumsum(jnp.flip(qg_all, 0), axis=0), 0) - qg_all).astype(jnp.bfloat16)
    causal = jnp.tril(jnp.ones((TOK_DEV, TOK_DEV), bool))

    def block_grads(items):
        q_blk, k_blk, v_blk, g_blk, prefix, suffix = items
        qf = q_blk.astype(jnp.float32)
        kf = k_blk.astype(jnp.float32)
        vf = v_blk.astype(jnp.float32)
        gf = g_blk.astype(jnp.float32)
        pf = prefix.astype(jnp.float32)
        sf = suffix.astype(jnp.float32)
        attn = jnp.where(causal[None], jnp.einsum('thi,shi->hts', qf, kf), 0.0).astype(jnp.bfloat16).astype(jnp.float32)
        back = jnp.where(causal[None], jnp.einsum('thj,shj->hts', gf, vf), 0.0).astype(jnp.bfloat16).astype(jnp.float32)
        out_rec = (scale * (jnp.einsum('hts,shj->thj', attn, vf) + jnp.einsum('thi,hij->thj', qf, pf))).astype(jnp.bfloat16)
        q_grad = (scale * (jnp.einsum('hts,shi->thi', back, kf) + jnp.einsum('thj,hij->thi', gf, pf))).astype(jnp.bfloat16)
        k_grad = (scale * (jnp.einsum('hts,thi->shi', back, qf) + jnp.einsum('shj,hij->shi', vf, sf))).astype(jnp.bfloat16)
        v_grad = (scale * (jnp.einsum('hts,thj->shj', attn, gf) + jnp.einsum('shi,hij->shj', kf, sf))).astype(jnp.bfloat16)
        return (out_rec, q_grad, k_grad, v_grad)
    out_rec, q_grad, k_grad, v_grad = lax.map(block_grads, (q_all, k_all, v_all, g_all, prefix_all, suffix_all))
    width = HEADS * HEAD_DIM
    out_rec = out_rec.reshape(TOKENS, width)
    weight_grad = jnp.dot(grad_out.T, out_rec, preferred_element_type=jnp.float32) * (1.0 / math.sqrt(TOKENS))
    return (q_grad.reshape(TOKENS, width), k_grad.reshape(TOKENS, width), v_grad.reshape(TOKENS, width), weight_grad)
```

```python
import math

import jax
import jax.numpy as jnp
from jax import lax
from jax.experimental import pallas as pl
from jax.experimental.pallas import tpu as pltpu
from jax.sharding import PartitionSpec as P

MESH = pl.DeviceIdType.MESH
F32, BF16 = jnp.float32, jnp.bfloat16
D = 128
T = 512
SCALE = 1.0 / math.sqrt(128 * 65536)
WSCALE = 1.0 / math.sqrt(65536)


def dot_nn(a, b):
    return lax.dot_general(a, b, (((1,), (0,)), ((), ())), preferred_element_type=F32)


def dot_nt(a, b):
    return lax.dot_general(a, b, (((1,), (1,)), ((), ())), preferred_element_type=F32)


def dot_tn(a, b):
    return lax.dot_general(a, b, (((0,), (0,)), ((), ())), preferred_element_type=F32)


def heads(body):
    def step(h, carry):
        body(h, pl.ds(pl.multiple_of(h * D, D), D))
        return carry

    lax.fori_loop(0, 4, step, 0)


def times(low, high, body):
    def step(i, carry):
        body(i)
        return carry

    lax.fori_loop(low, high, step, 0)


def kernel(
    q_in, k_in, v_in, g_in, w_in,
    q_out, k_out, v_out, w_out,
    q, k, v, gbuf, wown, wst, av, outb, agf, ag, kpart, vpart,
    sb, s1, s2s, s2, s3s, state,
    hf, rs, r1, hb, r2, h2, h2b, r3, h3, ra, fin, rc,
    wo,
    load_sem, store_sem,
    g_ss, g_rs, w0_ss, w0_rs, wa_ss, wa_rs, w2_ss, w2_rs, w3_ss, w3_rs, w4_ss, w4_rs,
    p1_ss, p1_rs, p2_ss, p2_rs, p3_ss, p3_rs,
    r1_ss, r1_rs, r2_ss, r2_rs, r3_ss, r3_rs, ra_ss, ra_rs, rc_ss, rc_rs,
):
    seq = lax.axis_index("seq")
    y = lax.axis_index("head")
    z, x, c = seq // 8, (seq // 2) % 4, seq % 2
    zq, zr = z // 4, z % 4
    group, m = seq // 16, seq % 16
    oc = 1 - c
    a2 = oc * zr + c * x
    a3 = oc * x + c * zr
    zstep = (0, 1, 2, 15)

    def dev(z_, x_, c_):
        return ((z_ * 4 + x_) * 2 + c_, y)

    def along(first, n):
        return dev(first * ((z + zstep[n]) % 16) + (1 - first) * z, first * x + (1 - first) * ((x + n) % 4), c)

    def peer2(n):
        return along(oc, n)

    def peer3(n):
        return along(c, n)

    def peer4(n):
        return dev((z + 4 * n) % 16, x, c)

    other = dev(z, x, oc)

    def remote(src, dst, ss, rs_, to):
        return pltpu.make_async_remote_copy(
            src_ref=src, dst_ref=dst, send_sem=ss, recv_sem=rs_, device_id=to, device_id_type=MESH
        )

    loads = [
        pltpu.make_async_copy(src, dst, load_sem.at[i])
        for i, (src, dst) in enumerate(((k_in, k), (v_in, v), (w_in, wown), (q_in, q), (g_in, gbuf.at[y])))
    ]
    for copy in loads:
        copy.start()

    barrier = pltpu.get_barrier_semaphore()

    def greet(to):
        pl.semaphore_signal(barrier, inc=1, device_id=to, device_id_type=MESH)

    times(1, 16, lambda n: greet((group * 16 + (m + n) % 16, y)))
    times(1, 8, lambda n: greet((((group + n) % 8) * 16 + m, y)))
    times(1, 4, lambda n: greet((seq, (y + n) % 4)))
    greet(dev((z + 1) % 16, x, c))
    greet(dev((z + 15) % 16, x, c))
    pl.semaphore_wait(barrier, 27)

    def g_copy(n):
        return remote(g_in, gbuf.at[y], g_ss.at[n - 1], g_rs.at[n - 1], (seq, (y + n) % 4))

    for n in (1, 3, 2):
        g_copy(n).start()

    loads[2].wait()
    w0 = remote(
        wown.at[:, pl.ds(pl.multiple_of(oc * 256, 256), 256)],
        wst.at[oc, zq, a2, a3, c],
        w0_ss, w0_rs, other,
    )
    w0.start()
    wst[c, zq, a3, a2, c] = wown[:, pl.ds(pl.multiple_of(c * 256, 256), 256)]

    loads[0].wait()
    loads[1].wait()

    def scan_piece1(i, n):
        to = (m + n) % 16
        return remote(sb.at[i, to], s1.at[i, m], p1_ss.at[i, n - 1], p1_rs.at[i, n - 1], (group * 16 + to, y))

    def scan_piece2(i, n):
        return remote(s2s.at[i], s2.at[i, group], p2_ss.at[i, n - 1], p2_rs.at[i, n - 1], (((group + n) % 8) * 16 + m, y))

    def scan_piece3(i, n):
        to = (m + n) % 16
        return remote(s3s.at[i, to], state.at[i, m], p3_ss.at[i, n - 1], p3_rs.at[i, n - 1], (group * 16 + to, y))

    def scan_send(i, a, b):
        def one(h, cols):
            s = dot_tn(a[:, cols], b[:, cols]).astype(BF16)
            sb[i, pl.ds(h * 4, 4)] = s.reshape(4, 32, D)

        heads(one)
        times(1, 16, lambda n: scan_piece1(i, n).start())
        s1[i, m] = sb[i, m]

    def scan_total(i):
        times(1, 16, lambda n: scan_piece1(i, n).wait_recv())
        total = s1[i, 0].astype(F32)
        for j in range(1, 16):
            total += s1[i, j].astype(F32)
        s2s[i] = total.astype(s2s.dtype)
        times(1, 8, lambda n: scan_piece2(i, n).start())
        s2[i, group] = jnp.zeros_like(s2[i, group])

    def scan_back(i):
        times(1, 8, lambda n: scan_piece2(i, n).wait_recv())
        run = jnp.zeros((32, D), F32)
        for j in range(8):
            counts = (j < group) if i == 0 else (j > group)
            run += jnp.where(counts, s2[i, j].astype(F32), 0.0)
        for j in range(16) if i == 0 else range(15, -1, -1):
            s3s[i, j] = run.astype(BF16)
            run += s1[i, j].astype(F32)
        times(1, 16, lambda n: scan_piece3(i, n).start())
        state[i, m] = s3s[i, m]

    def scan_get(i):
        times(1, 16, lambda n: scan_piece3(i, n).wait_recv())

    def state_of(i, h):
        return state[i, pl.ds(h * 4, 4)].reshape(D, D)

    scan_send(0, k, v)

    w0.wait_recv()

    def wa_copy(n):
        part = wst.at[c, zq, a3, a2]
        return remote(part, part, wa_ss.at[n - 1], wa_rs.at[n - 1], peer4(n))

    for n in (2, 1, 3):
        wa_copy(n).start()

    loads[3].wait()

    def lower(n, height):
        row = lax.broadcasted_iota(jnp.int32, (D, n), 0) + height
        col = lax.broadcasted_iota(jnp.int32, (D, n), 1)
        return row >= col

    def upper(n):
        row = lax.broadcasted_iota(jnp.int32, (D, n), 0)
        col = lax.broadcasted_iota(jnp.int32, (D, n), 1)
        return col >= row

    def attend(h, cols):
        for r in range(4):
            n = (r + 1) * D
            rows = slice(r * D, n)
            s = dot_nt(q[rows, cols], k[:n, cols])
            s = jnp.where(lower(n, r * D), s, 0.0).astype(BF16)
            av[rows, cols] = dot_nn(s, v[:n, cols])

    heads(attend)

    scan_total(0)

    def w2_copy(n):
        part = wst.at[c, :, a3, a2]
        return remote(part, part, w2_ss.at[n - 1], w2_rs.at[n - 1], peer2(n))

    def w3_copy(n):
        part = wst.at[c, :, a3]
        return remote(part, part, w3_ss.at[n - 1], w3_rs.at[n - 1], peer3(n))

    def w4_copy(n):
        part = wst.at[c, :, (a3 + n) % 4]
        return remote(part, part, w4_ss.at[n], w4_rs.at[n], other)

    for n in (1, 2, 3):
        wa_copy(n).wait_recv()
    for n in (1, 3, 2):
        w2_copy(n).start()
    for n in (1, 3, 2):
        w2_copy(n).wait_recv()
    for n in (1, 3, 2):
        w3_copy(n).start()
    w4_copy(0).start()

    scan_back(0)

    for n in (1, 3, 2):
        w3_copy(n).wait_recv()
        w4_copy((4 - n) % 4).start()

    scan_get(0)

    def rec(h, cols):
        outb[:, cols] = (SCALE * (av[:, cols] + dot_nn(q[:, cols], state_of(0, h)))).astype(BF16)

    heads(rec)

    loads[4].wait()
    for n in (1, 3, 2):
        g_copy(n).wait_recv()

    def r1_copy(i):
        return remote(rs.at[i], r1.at[i], r1_ss.at[i], r1_rs.at[i], other)

    def contribute(i):
        mine = dot_tn(gbuf[i], outb[:, pl.ds(pl.multiple_of(c * 256, 256), 256)])
        theirs = dot_tn(gbuf[i], outb[:, pl.ds(pl.multiple_of(oc * 256, 256), 256)])
        for zi in range(4):
            for xi in range(4):
                rows = slice((zi * 4 + xi) * 32, (zi * 4 + xi) * 32 + 32)
                of_x, of_z = oc * xi + c * zi, oc * zi + c * xi
                hf[i, of_x, of_z] = mine[rows].reshape(2, 16, 256)
                rs[i, of_z, of_x] = theirs[rows].reshape(2, 16, 256).astype(BF16)
        r1_copy(i).start()

    times(0, 4, contribute)

    for n in range(4):
        w4_copy(n).wait_recv()

    agf[...] = jnp.zeros_like(agf)

    def project(i):
        for half in range(2):
            order = [(xi, zi) if half == 0 else (zi, xi) for zi in range(4) for xi in range(4)]
            w = jnp.concatenate([wst[half, i, u, t].reshape(32, 256) for u, t in order], axis=0)
            agf[:, half * 256 : half * 256 + 256] += dot_nn(gbuf[i], w)

    times(0, 4, project)
    ag[...] = agf[...].astype(BF16)

    scan_send(1, q, ag)

    def r2_copy(n):
        return remote(hb.at[:, (a3 + n) % 4], r2.at[n - 1], r2_ss.at[n - 1], r2_rs.at[n - 1], peer3(n))

    def pair(i):
        r1_copy(i).wait_recv()
        for u in range(4):
            total = hf[i, u] + r1[i, u].astype(F32)
            hf[i, u] = total
            hb[i, u] = total.astype(BF16)

    times(0, 4, pair)
    for n in (1, 3, 2):
        r2_copy(n).start()

    def back(h, cols):
        for r in range(4):
            n = (r + 1) * D
            rows = slice(r * D, n)
            s = dot_nt(ag[rows, cols], v[:n, cols])
            s = jnp.where(lower(n, r * D), s, 0.0).astype(BF16)
            total = dot_nn(s, k[:n, cols]) + dot_nt(ag[rows, cols], state_of(0, h))
            outb[rows, cols] = (SCALE * total).astype(BF16)

    def back_kv(h, cols):
        for r in range(4):
            rows = slice(r * D, (r + 1) * D)
            mask = upper(T - r * D)
            s = dot_nt(v[rows, cols], ag[r * D :, cols])
            s = jnp.where(mask, s, 0.0).astype(BF16)
            kpart[rows, cols] = dot_nn(s, q[r * D :, cols])
            s = dot_nt(k[rows, cols], q[r * D :, cols])
            s = jnp.where(mask, s, 0.0).astype(BF16)
            vpart[rows, cols] = dot_nn(s, ag[r * D :, cols])

    heads(back)
    q_store = pltpu.make_async_copy(outb, q_out, store_sem.at[0])
    q_store.start()
    scan_total(1)
    heads(back_kv)

    def r3_copy(n):
        return remote(h2b.at[:, (a2 + n) % 4], r3.at[n - 1], r3_ss.at[n - 1], r3_rs.at[n - 1], peer2(n))

    for n in (1, 3, 2):
        r2_copy(n).wait_recv()

    def third(i):
        total = hf[i, a3]
        for n in range(3):
            total += r2[n, i].astype(F32)
        h2[i] = total
        h2b[i] = total.astype(BF16)

    times(0, 4, third)
    for n in (1, 3, 2):
        r3_copy(n).start()

    scan_back(1)

    def ra_copy(n):
        return remote(h3.at[(zq + n) % 4], ra.at[n - 1], ra_ss.at[n - 1], ra_rs.at[n - 1], peer4(n))

    for n in (1, 3, 2):
        r3_copy(n).wait_recv()
    for i in range(4):
        total = h2[i, a2]
        for n in range(3):
            total += r3[n, i].astype(F32)
        h3[i] = total
    for n in (2, 1, 3):
        ra_copy(n).start()

    scan_get(1)

    q_store.wait()

    def final(h, cols):
        suffix = state_of(1, h)
        outb[:, cols] = (SCALE * (kpart[:, cols] + dot_nt(v[:, cols], suffix))).astype(BF16)
        ag[:, cols] = (SCALE * (vpart[:, cols] + dot_nn(k[:, cols], suffix))).astype(BF16)

    heads(final)
    k_store = pltpu.make_async_copy(outb, k_out, store_sem.at[1])
    v_store = pltpu.make_async_copy(ag, v_out, store_sem.at[2])
    k_store.start()
    v_store.start()

    for n in (1, 2, 3):
        ra_copy(n).wait_recv()
    total = h3[zq]
    for n in range(3):
        total += ra[n]
    fin[...] = total * WSCALE
    rc_copy = remote(fin.at[oc], rc, rc_ss, rc_rs, other)
    rc_copy.start()
    wo[:, pl.ds(pl.multiple_of(c * 256, 256), 256)] = fin[c]
    rc_copy.wait_recv()
    wo[:, pl.ds(pl.multiple_of(oc * 256, 256), 256)] = rc[...]
    w_store = pltpu.make_async_copy(wo, w_out, store_sem.at[3])
    w_store.start()

    w0.wait_send()
    for n in (1, 2, 3):
        g_copy(n).wait_send()
        wa_copy(n).wait_send()
        w2_copy(n).wait_send()
        w3_copy(n).wait_send()
        r2_copy(n).wait_send()
        r3_copy(n).wait_send()
        ra_copy(n).wait_send()
    for n in range(4):
        w4_copy(n).wait_send()
    times(0, 4, lambda i: r1_copy(i).wait_send())
    for i in range(2):
        times(1, 16, lambda n, i=i: scan_piece1(i, n).wait_send())
        times(1, 8, lambda n, i=i: scan_piece2(i, n).wait_send())
        times(1, 16, lambda n, i=i: scan_piece3(i, n).wait_send())
    rc_copy.wait_send()
    k_store.wait()
    v_store.wait()
    w_store.wait()


def per_device(queries, keys, values, grad_out, out_weight):
    def vmem(*shape, dtype=BF16):
        return pltpu.VMEM(shape, dtype)

    def sems(*shape):
        return [pltpu.SemaphoreType.DMA(shape)] * 2

    wide = (T, T)
    scratch = [
        vmem(*wide), vmem(*wide), vmem(*wide),
        vmem(4, *wide),
        vmem(16, 512),
        vmem(2, 4, 4, 4, 2, 16, 256),
        vmem(*wide, dtype=F32),
        vmem(*wide),
        vmem(*wide, dtype=F32),
        vmem(*wide),
        vmem(*wide, dtype=F32), vmem(*wide, dtype=F32),
        vmem(2, 16, 32, D), vmem(2, 16, 32, D),
        vmem(2, 32, D), vmem(2, 8, 32, D),
        vmem(2, 16, 32, D), vmem(2, 16, 32, D),
        vmem(4, 4, 4, 2, 16, 256, dtype=F32),
        vmem(4, 4, 4, 2, 16, 256),
        vmem(4, 4, 4, 2, 16, 256),
        vmem(4, 4, 4, 2, 16, 256),
        vmem(3, 4, 4, 2, 16, 256),
        vmem(4, 4, 2, 16, 256, dtype=F32),
        vmem(4, 4, 2, 16, 256),
        vmem(3, 4, 2, 16, 256),
        vmem(4, 2, 16, 256, dtype=F32),
        vmem(3, 2, 16, 256, dtype=F32),
        vmem(2, 16, 256, dtype=F32),
        vmem(16, 256, dtype=F32),
        vmem(16, 512, dtype=F32),
        pltpu.SemaphoreType.DMA((5,)), pltpu.SemaphoreType.DMA((4,)),
        *sems(3),
        pltpu.SemaphoreType.DMA, pltpu.SemaphoreType.DMA,
        *sems(3), *sems(3), *sems(3), *sems(4),
        *sems(2, 15), *sems(2, 7), *sems(2, 15),
        *sems(4), *sems(3), *sems(3), *sems(3),
        pltpu.SemaphoreType.DMA, pltpu.SemaphoreType.DMA,
    ]
    shape = jax.ShapeDtypeStruct(wide, BF16)
    return pl.pallas_call(
        kernel,
        out_shape=(shape, shape, shape, jax.ShapeDtypeStruct((16, 512), F32)),
        in_specs=[pl.BlockSpec(memory_space=pl.ANY)] * 5,
        out_specs=[pl.BlockSpec(memory_space=pl.ANY)] * 4,
        scratch_shapes=scratch,
        compiler_params=pltpu.CompilerParams(
            collective_id=0, has_side_effects=True, vmem_limit_bytes=56 * 2**20
        ),
        name="attention_backward",
    )(queries, keys, values, grad_out, out_weight)


def solution(mesh):
    spec = P("seq", "head")
    return jax.shard_map(
        per_device, mesh=mesh, in_specs=(spec,) * 5, out_specs=(spec,) * 4, check_vma=False
    )
```

```python
import math

import jax
import jax.numpy as jnp
from jax import lax
from jax.experimental import pallas as pl
from jax.experimental.pallas import tpu as pltpu
from jax.sharding import PartitionSpec as P

MESH = pl.DeviceIdType.MESH
F32, BF16 = jnp.float32, jnp.bfloat16
D = 128
T = 512
SCALE = 1.0 / math.sqrt(128 * 65536)
WSCALE = 1.0 / math.sqrt(65536)


def dot_nn(a, b):
    return lax.dot_general(a, b, (((1,), (0,)), ((), ())), preferred_element_type=F32)


def dot_nt(a, b):
    return lax.dot_general(a, b, (((1,), (1,)), ((), ())), preferred_element_type=F32)


def dot_tn(a, b):
    return lax.dot_general(a, b, (((0,), (0,)), ((), ())), preferred_element_type=F32)


def heads(body):
    def step(h, carry):
        body(h, pl.ds(pl.multiple_of(h * D, D), D))
        return carry

    lax.fori_loop(0, 4, step, 0)


def each_head(body):
    for h in range(4):
        body(h, slice(h * D, h * D + D))


def times(low, high, body):
    def step(i, carry):
        body(i)
        return carry

    lax.fori_loop(low, high, step, 0)


def kernel(
    q_in, k_in, v_in, g_in, w_in,
    q_out, k_out, v_out, w_out,
    q, k, v, gbuf, gt, qt, wown, wst, av, at, outb, ag, kpart, vpart,
    sb, s1, s2s, s2, s3s, state,
    hf, rs, r1, hb, r2, h2, h2b, r3, h3, ra, rb,
    wo,
    load_sem, store_sem,
    g_ss, g_rs, w0_ss, w0_rs, wa_ss, wa_rs, wb_ss, wb_rs, w2_ss, w2_rs, w3_ss, w3_rs, w4_ss, w4_rs,
    p1_ss, p1_rs, p2_ss, p2_rs, p3_ss, p3_rs,
    r1_ss, r1_rs, r2_ss, r2_rs, r3_ss, r3_rs, ra_ss, ra_rs, rb_ss, rb_rs,
):
    seq = lax.axis_index("seq")
    y = lax.axis_index("head")
    z, x, c = seq // 8, (seq // 2) % 4, seq % 2
    zq, zr = z // 4, z % 4
    group, m = seq // 16, seq % 16
    oc = 1 - c
    a2 = oc * zr + c * x
    a3 = oc * x + c * zr
    zstep = (0, 1, 2, 15, 14)
    hops = ((1, slice(0, 4)), (3, slice(0, 4)), (2, slice(0, 2)), (4, slice(2, 4)))

    def dev(z_, x_, c_):
        return ((z_ * 4 + x_) * 2 + c_, y)

    def along(first, n):
        by_x = (x + (2 if n == 4 else n)) % 4
        return dev(first * ((z + zstep[n]) % 16) + (1 - first) * z, first * x + (1 - first) * by_x, c)

    def peer2(n):
        return along(oc, n)

    def peer3(n):
        return along(c, n)

    def peer4(n, core=c):
        return dev((z + 4 * n) % 16, x, core)

    other = dev(z, x, oc)

    def remote(src, dst, ss, rs_, to):
        return pltpu.make_async_remote_copy(
            src_ref=src, dst_ref=dst, send_sem=ss, recv_sem=rs_, device_id=to, device_id_type=MESH
        )

    loads = [
        pltpu.make_async_copy(src, dst, load_sem.at[i])
        for i, (src, dst) in enumerate(((k_in, k), (v_in, v), (w_in, wown), (q_in, q), (g_in, gbuf.at[y])))
    ]
    for copy in loads:
        copy.start()

    barrier = pltpu.get_barrier_semaphore()

    def greet(to):
        pl.semaphore_signal(barrier, inc=1, device_id=to, device_id_type=MESH)

    times(1, 8, lambda n: greet((((group + n) % 8) * 16 + m, y)))
    times(1, 16, lambda n: greet((group * 16 + (m + n) % 16, y)))
    times(1, 4, lambda n: greet((seq, (y + n) % 4)))
    greet(dev((z + 1) % 16, x, c))
    greet(dev((z + 15) % 16, x, c))
    for n in (1, 2, 3):
        greet(peer4(n, oc))

    own = pl.ds(pl.multiple_of(c * 256, 256), 256)
    others = pl.ds(pl.multiple_of(oc * 256, 256), 256)

    top, bottom = slice(0, 256), slice(256, 512)

    def g_copy(i):
        owner, rows, n = (
            (y, top, 1), (y, bottom, 3), (y, bottom, 1), (y, top, 3),
            ((y + 3) % 4, top, 1), ((y + 1) % 4, bottom, 3),
        )[i]
        part = gbuf.at[owner, rows]
        return remote(part, part, g_ss.at[i], g_rs.at[i], (seq, (y + n) % 4))

    def wa_copy(n):
        return remote(wown.at[:, own], wst.at[c, zq, a3, a2, c], wa_ss.at[n - 1], wa_rs.at[n - 1], peer4(n))

    def wb_copy(n):
        return remote(wown.at[:, others], wst.at[oc, zq, a2, a3, c], wb_ss.at[n - 1], wb_rs.at[n - 1], peer4(n, oc))

    w0 = remote(wown.at[:, others], wst.at[oc, zq, a2, a3, c], w0_ss, w0_rs, other)

    def scan_piece1(i, n):
        to = (m + n) % 16
        return remote(sb.at[i, to], s1.at[i, m], p1_ss.at[i, n - 1], p1_rs.at[i, n - 1], (group * 16 + to, y))

    def scan_piece2(i, n):
        return remote(s2s.at[i], s2.at[i, group], p2_ss.at[i, n - 1], p2_rs.at[i, n - 1], (((group + n) % 8) * 16 + m, y))

    def scan_piece3(i, n):
        to = (m + n) % 16
        return remote(s3s.at[i, to], state.at[i, m], p3_ss.at[i, n - 1], p3_rs.at[i, n - 1], (group * 16 + to, y))

    def scan_own(i, product):
        def one(h, cols):
            s = product(cols).astype(BF16)
            sb[i, h * 4 : h * 4 + 4] = s.reshape(4, 32, D)

        each_head(one)
        s1[i, m] = sb[i, m]

    def scan_start(i):
        times(1, 16, lambda n: scan_piece1(i, n).start())

    def scan_total(i):
        times(1, 16, lambda n: scan_piece1(i, n).wait_recv())
        total = s1[i, 0].astype(F32)
        for j in range(1, 16):
            total += s1[i, j].astype(F32)
        s2s[i] = total.astype(s2s.dtype)
        times(1, 8, lambda n: scan_piece2(i, n).start())
        s2[i, group] = jnp.zeros_like(s2[i, group])

    def scan_back(i):
        times(1, 8, lambda n: scan_piece2(i, n).wait_recv())
        run = jnp.zeros((32, D), F32)
        for j in range(8):
            counts = (j < group) if i == 0 else (j > group)
            run += jnp.where(counts, s2[i, j].astype(F32), 0.0)
        for j in range(16) if i == 0 else range(15, -1, -1):
            s3s[i, j] = run.astype(BF16)
            run += s1[i, j].astype(F32)
        times(1, 16, lambda n: scan_piece3(i, n).start())
        state[i, m] = s3s[i, m]

    def scan_get(i):
        times(1, 16, lambda n: scan_piece3(i, n).wait_recv())

    def state_of(i, h):
        return state[i, pl.ds(h * 4, 4)].reshape(D, D)

    loads[0].wait()
    loads[1].wait()
    scan_own(0, lambda cols: dot_tn(k[:, cols], v[:, cols]))
    loads[2].wait()
    wst[c, zq, a3, a2, c] = wown[:, own]

    pl.semaphore_wait(barrier, 30)

    for n in (2, 1, 3):
        wa_copy(n).start()
        wb_copy(n).start()
    w0.start()
    scan_start(0)
    loads[4].wait()
    for i in range(4):
        g_copy(i).start()
    loads[3].wait()

    def lower(n, height):
        row = lax.broadcasted_iota(jnp.int32, (D, n), 0) + height
        col = lax.broadcasted_iota(jnp.int32, (D, n), 1)
        return row >= col

    def upper(n):
        row = lax.broadcasted_iota(jnp.int32, (D, n), 0)
        col = lax.broadcasted_iota(jnp.int32, (D, n), 1)
        return col >= row

    def attend(h, cols):
        for r in range(4):
            n = (r + 1) * D
            rows = slice(r * D, n)
            s = dot_nt(q[rows, cols], k[:n, cols])
            s = jnp.where(lower(n, r * D), s, 0.0).astype(BF16)
            av[rows, cols] = dot_nn(s, v[:n, cols])

    heads(attend)

    scan_total(0)

    for i in range(2):
        g_copy(i).wait_recv()
        g_copy(i + 4).start()

    def w2_copy(n, zs):
        part = wst.at[c, zs, a3, a2]
        return remote(part, part, w2_ss.at[n - 1], w2_rs.at[n - 1], peer2(n))

    def w3_copy(d, n, zs):
        part = wst.at[c, zs, a3, (a2 + d) % 4]
        return remote(part, part, w3_ss.at[d, n - 1], w3_rs.at[d, n - 1], peer3(n))

    def w4_copy(d, e):
        part = wst.at[c, :, (a3 + e) % 4, (a2 + d) % 4]
        return remote(part, part, w4_ss.at[d, e], w4_rs.at[d, e], other)

    def w3_start(d):
        for n, zs in hops:
            w3_copy(d, n, zs).start()
        w4_copy(d, 0).start()

    w0.wait_recv()
    for n in (1, 3, 2):
        wa_copy(n).wait_recv()
        wb_copy(n).wait_recv()
    for n, zs in hops:
        w2_copy(n, zs).start()
    w3_start(0)
    qt[...] = q[...].T
    gt[y] = gbuf[y].T
    for n, zs in hops:
        w2_copy(n, zs).wait_recv()
        if n != 2:
            w3_start(4 - n or 2)

    def attend_t(h, cols):
        for r in range(4):
            rows = slice(r * D, (r + 1) * D)
            s = dot_nt(k[rows, cols], q[r * D :, cols])
            at[h, rows, r * D :] = jnp.where(upper(T - r * D), s, 0.0).astype(BF16)

    heads(attend_t)

    scan_back(0)

    for d in (0, 3, 1, 2):
        for n, zs in hops:
            w3_copy(d, n, zs).wait_recv()
            if n != 2:
                w4_copy(d, 4 - n or 2).start()

    for i in range(2, 6):
        g_copy(i).wait_recv()
    for n in (1, 3, 2):
        gt[(y + n) % 4] = gbuf[(y + n) % 4].T

    scan_get(0)

    def rec(h, cols):
        outb[:, cols] = (SCALE * (av[:, cols] + dot_nn(q[:, cols], state_of(0, h)))).astype(BF16)

    each_head(rec)

    def r1_copy(i):
        return remote(rs.at[i], r1.at[i], r1_ss.at[i], r1_rs.at[i], other)

    def contribute(i):
        mine = dot_nn(gt[i], outb[:, own])
        theirs = dot_nn(gt[i], outb[:, others])
        for zi in range(4):
            for xi in range(4):
                rows = slice((zi * 4 + xi) * 32, (zi * 4 + xi) * 32 + 32)
                of_x, of_z = oc * xi + c * zi, oc * zi + c * xi
                hf[i, of_x, of_z] = mine[rows].reshape(2, 16, 256)
                rs[i, of_z, of_x] = theirs[rows].reshape(2, 16, 256).astype(BF16)
        r1_copy(i).start()

    times(0, 4, contribute)

    def project(half, cols):
        first = 1 - half
        total = None
        for i in range(4):
            w = [
                wst[half, i, first * xi + half * zi, first * zi + half * xi].reshape(32, 256)
                for zi in range(4)
                for xi in range(4)
            ]
            part = dot_nn(gbuf[i], jnp.concatenate(w, axis=0))
            total = part if total is None else total + part
        ag[:, cols] = total.astype(BF16)

    project(c, own)
    for d in range(4):
        for e in range(4):
            w4_copy(d, e).wait_recv()
    project(oc, others)

    scan_own(1, lambda cols: dot_nn(qt[cols], ag[:, cols]))
    scan_start(1)

    def r2_copy(p, d, n):
        to = peer3(4 if n == 2 and p == 1 else n)
        part = (a2 + d) % 4
        zs = slice(2 * p, 2 * p + 2)
        return remote(
            hb.at[n - 1, part, zs], r2.at[n - 1, part, zs], r2_ss.at[p, d, n - 1], r2_rs.at[p, d, n - 1], to
        )

    for p in range(2):
        for i in (2 * p, 2 * p + 1):
            r1_copy(i).wait_recv()
            for n in (1, 3, 2):
                u = (a3 + n) % 4
                hb[n - 1, :, i] = (hf[i, u] + r1[i, u].astype(F32)).astype(BF16)
            h2[:, i] = hf[i, a3] + r1[i, a3].astype(F32)
        for d in (1, 3, 2, 0):
            for n in (1, 3, 2):
                r2_copy(p, d, n).start()

    def back(h, cols):
        for r in range(4):
            n = (r + 1) * D
            rows = slice(r * D, n)
            s = dot_nt(ag[rows, cols], v[:n, cols])
            s = jnp.where(lower(n, r * D), s, 0.0).astype(BF16)
            total = dot_nn(s, k[:n, cols]) + dot_nt(ag[rows, cols], state_of(0, h))
            outb[rows, cols] = (SCALE * total).astype(BF16)

    def back_kv(h, cols):
        for r in range(4):
            rows = slice(r * D, (r + 1) * D)
            mask = upper(T - r * D)
            s = dot_nt(v[rows, cols], ag[r * D :, cols])
            s = jnp.where(mask, s, 0.0).astype(BF16)
            kpart[rows, cols] = dot_nn(s, q[r * D :, cols])
            vpart[rows, cols] = dot_nn(at[h, rows, r * D :], ag[r * D :, cols])

    heads(back)
    q_store = pltpu.make_async_copy(outb, q_out, store_sem.at[0])
    q_store.start()
    scan_total(1)
    heads(back_kv)

    def r3_copy(n, zs):
        slot = (n if n < 4 else 2) - 1
        return remote(h2b.at[slot, zs], r3.at[slot, zs], r3_ss.at[n - 1], r3_rs.at[n - 1], peer2(n))

    for d in (1, 3, 2, 0):
        part = (a2 + d) % 4
        total = h2[part]
        for n in (1, 3, 2):
            for p in range(2):
                r2_copy(p, d, n).wait_recv()
            total += r2[n - 1, part].astype(F32)
        if d:
            h2b[d - 1] = total.astype(BF16)
            for n, zs in hops:
                if n == d or n == d + 2 == 4:
                    r3_copy(n, zs).start()
        else:
            h2[part] = total

    scan_back(1)

    def ra_copy(n):
        return remote(h3.at[(zq + n) % 4, c], ra.at[n - 1], ra_ss.at[n - 1], ra_rs.at[n - 1], peer4(n))

    def rb_copy(n):
        return remote(h3.at[(zq + n) % 4, oc], rb.at[n], rb_ss.at[n], rb_rs.at[n], peer4(n, oc) if n else other)

    for n, zs in hops:
        r3_copy(n, zs).wait_recv()
    for i in range(4):
        total = h2[a2, i]
        for n in range(3):
            total += r3[n, i].astype(F32)
        h3[i] = total
    for n in (2, 1, 3):
        ra_copy(n).start()
        rb_copy(n).start()
    rb_copy(0).start()

    scan_get(1)

    q_store.wait()

    def final_k(h, cols):
        outb[:, cols] = (SCALE * (kpart[:, cols] + dot_nt(v[:, cols], state_of(1, h)))).astype(BF16)

    def final_v(h, cols):
        ag[:, cols] = (SCALE * (vpart[:, cols] + dot_nn(k[:, cols], state_of(1, h)))).astype(BF16)

    k_store = pltpu.make_async_copy(outb, k_out, store_sem.at[1])
    v_store = pltpu.make_async_copy(ag, v_out, store_sem.at[2])
    each_head(final_k)
    k_store.start()
    each_head(final_v)
    v_store.start()

    mine = h3[zq, c]
    for n in range(3):
        ra_copy(n + 1).wait_recv()
        mine += ra[n]
    wo[:, own] = mine * WSCALE
    rb_copy(0).wait_recv()
    theirs = rb[0]
    for n in range(1, 4):
        rb_copy(n).wait_recv()
        theirs += rb[n]
    wo[:, others] = theirs * WSCALE
    w_store = pltpu.make_async_copy(wo, w_out, store_sem.at[3])
    w_store.start()

    w0.wait_send()
    for n, zs in hops:
        w2_copy(n, zs).wait_send()
        r3_copy(n, zs).wait_send()
        for d in range(4):
            w3_copy(d, n, zs).wait_send()
    for n in (1, 2, 3):
        wa_copy(n).wait_send()
        wb_copy(n).wait_send()
        ra_copy(n).wait_send()
    for n in range(4):
        rb_copy(n).wait_send()
        r1_copy(n).wait_send()
        for d in range(4):
            w4_copy(d, n).wait_send()
    for p in range(2):
        for d in range(4):
            for n in (1, 2, 3):
                r2_copy(p, d, n).wait_send()
    for i in range(6):
        g_copy(i).wait_send()
    for i in range(2):
        times(1, 16, lambda n, i=i: scan_piece1(i, n).wait_send())
        times(1, 8, lambda n, i=i: scan_piece2(i, n).wait_send())
        times(1, 16, lambda n, i=i: scan_piece3(i, n).wait_send())
    k_store.wait()
    v_store.wait()
    w_store.wait()


def hand_over(*refs):
    ins, outs, held, sem = refs[:4], refs[4:8], refs[8:12], refs[12]
    reads = [pltpu.make_async_copy(ins[i], held[i], sem.at[0, i]) for i in range(4)]
    writes = [pltpu.make_async_copy(held[i], outs[i], sem.at[1, i]) for i in range(4)]
    for read in reads:
        read.start()
    for read, write in zip(reads, writes):
        read.wait()
        write.start()
    for write in writes:
        write.wait()


def per_device(queries, keys, values, grad_out, out_weight):
    def vmem(*shape, dtype=BF16):
        return pltpu.VMEM(shape, dtype)

    def sems(*shape):
        return [pltpu.SemaphoreType.DMA(shape)] * 2

    wide = (T, T)
    scratch = [
        vmem(*wide), vmem(*wide), vmem(*wide),
        vmem(4, *wide), vmem(4, *wide), vmem(*wide),
        vmem(16, 512),
        vmem(2, 4, 4, 4, 2, 16, 256),
        vmem(*wide, dtype=F32),
        vmem(4, *wide),
        vmem(*wide),
        vmem(*wide),
        vmem(*wide, dtype=F32), vmem(*wide, dtype=F32),
        vmem(2, 16, 32, D), vmem(2, 16, 32, D),
        vmem(2, 32, D), vmem(2, 8, 32, D),
        vmem(2, 16, 32, D), vmem(2, 16, 32, D),
        vmem(4, 4, 4, 2, 16, 256, dtype=F32),
        vmem(4, 4, 4, 2, 16, 256),
        vmem(4, 4, 4, 2, 16, 256),
        vmem(3, 4, 4, 2, 16, 256),
        vmem(3, 4, 4, 2, 16, 256),
        vmem(4, 4, 2, 16, 256, dtype=F32),
        vmem(3, 4, 2, 16, 256),
        vmem(3, 4, 2, 16, 256),
        vmem(4, 2, 16, 256, dtype=F32),
        vmem(3, 16, 256, dtype=F32),
        vmem(4, 16, 256, dtype=F32),
        vmem(16, 512, dtype=F32),
        pltpu.SemaphoreType.DMA((5,)), pltpu.SemaphoreType.DMA((4,)),
        *sems(6),
        pltpu.SemaphoreType.DMA, pltpu.SemaphoreType.DMA,
        *sems(3), *sems(3), *sems(4), *sems(4, 4), *sems(4, 4),
        *sems(2, 15), *sems(2, 7), *sems(2, 15),
        *sems(4), *sems(2, 4, 3), *sems(4), *sems(3), *sems(4),
    ]
    shape = jax.ShapeDtypeStruct(wide, BF16)
    outs = pl.pallas_call(
        kernel,
        out_shape=(shape, shape, shape, jax.ShapeDtypeStruct((16, 512), F32)),
        in_specs=[pl.BlockSpec(memory_space=pl.ANY)] * 5,
        out_specs=[pl.BlockSpec(memory_space=pl.ANY)] * 4,
        scratch_shapes=scratch,
        compiler_params=pltpu.CompilerParams(
            collective_id=0, has_side_effects=True, vmem_limit_bytes=56 * 2**20
        ),
        name="attention_backward",
    )(queries, keys, values, grad_out, out_weight)
    return pl.pallas_call(
        hand_over,
        out_shape=tuple(jax.ShapeDtypeStruct(a.shape, a.dtype) for a in outs),
        in_specs=[pl.BlockSpec(memory_space=pl.ANY)] * 4,
        out_specs=[pl.BlockSpec(memory_space=pl.ANY)] * 4,
        scratch_shapes=[vmem(*a.shape, dtype=a.dtype) for a in outs] + [pltpu.SemaphoreType.DMA((2, 4))],
        name="hand_over",
    )(*outs)


def solution(mesh):
    spec = P("seq", "head")
    return jax.shard_map(
        per_device, mesh=mesh, in_specs=(spec,) * 5, out_specs=(spec,) * 4, check_vma=False
    )
```

```python
import math

import jax
import jax.numpy as jnp
from jax import lax
from jax.experimental import pallas as pl
from jax.experimental.pallas import tpu as pltpu
from jax.sharding import PartitionSpec as P

MESH = pl.DeviceIdType.MESH
F32, BF16 = jnp.float32, jnp.bfloat16
D = 128
T = 512
SCALE = 1.0 / math.sqrt(128 * 65536)
WSCALE = 1.0 / math.sqrt(65536)


def dot_nn(a, b):
    return lax.dot_general(a, b, (((1,), (0,)), ((), ())), preferred_element_type=F32)


def dot_nt(a, b):
    return lax.dot_general(a, b, (((1,), (1,)), ((), ())), preferred_element_type=F32)


def dot_tn(a, b):
    return lax.dot_general(a, b, (((0,), (0,)), ((), ())), preferred_element_type=F32)


def heads(body):
    def step(h, carry):
        body(h, pl.ds(pl.multiple_of(h * D, D), D))
        return carry

    lax.fori_loop(0, 4, step, 0)


def each_head(body):
    for h in range(4):
        body(h, slice(h * D, h * D + D))


def times(low, high, body):
    def step(i, carry):
        body(i)
        return carry

    lax.fori_loop(low, high, step, 0)


def kernel(
    q_in, k_in, v_in, g_in, w_in,
    q_out, k_out, v_out, w_out,
    q, k, v, gbuf, gt, qt, wown, wst, av, at, outb, ag, kpart, vpart,
    sb, s1, s2s, s2, s3s, state,
    hf, rs, r1, hb, r2, h2, h2b, r3, h3, ra, rb,
    wo,
    load_sem, store_sem,
    g_ss, g_rs, w0_ss, w0_rs, wa_ss, wa_rs, wb_ss, wb_rs, w2_ss, w2_rs, w3_ss, w3_rs, w4_ss, w4_rs,
    p1_ss, p1_rs, p2_ss, p2_rs, p3_ss, p3_rs,
    r1_ss, r1_rs, r2_ss, r2_rs, r3_ss, r3_rs, ra_ss, ra_rs, rb_ss, rb_rs,
):
    seq = lax.axis_index("seq")
    y = lax.axis_index("head")
    z, x, c = seq // 8, (seq // 2) % 4, seq % 2
    zq, zr = z // 4, z % 4
    group, m = seq // 16, seq % 16
    oc = 1 - c
    a2 = oc * zr + c * x
    a3 = oc * x + c * zr
    zstep = (0, 1, 2, 15, 14)
    hops = ((1, slice(0, 4)), (3, slice(0, 4)), (2, slice(0, 2)), (4, slice(2, 4)))

    def dev(z_, x_, c_):
        return ((z_ * 4 + x_) * 2 + c_, y)

    def along(first, n):
        by_x = (x + (2 if n == 4 else n)) % 4
        return dev(first * ((z + zstep[n]) % 16) + (1 - first) * z, first * x + (1 - first) * by_x, c)

    def peer2(n):
        return along(oc, n)

    def peer3(n):
        return along(c, n)

    def peer4(n, core=c):
        return dev((z + 4 * n) % 16, x, core)

    other = dev(z, x, oc)

    def remote(src, dst, ss, rs_, to):
        return pltpu.make_async_remote_copy(
            src_ref=src, dst_ref=dst, send_sem=ss, recv_sem=rs_, device_id=to, device_id_type=MESH
        )

    loads = [
        pltpu.make_async_copy(src, dst, load_sem.at[i])
        for i, (src, dst) in enumerate(((k_in, k), (v_in, v), (w_in, wown), (q_in, q), (g_in, gbuf.at[y])))
    ]
    for copy in loads:
        copy.start()

    barrier = pltpu.get_barrier_semaphore()

    def greet(to):
        pl.semaphore_signal(barrier, inc=1, device_id=to, device_id_type=MESH)

    times(1, 8, lambda n: greet((((group + n) % 8) * 16 + m, y)))
    times(1, 16, lambda n: greet((group * 16 + (m + n) % 16, y)))
    times(1, 4, lambda n: greet((seq, (y + n) % 4)))
    greet(dev((z + 1) % 16, x, c))
    greet(dev((z + 15) % 16, x, c))
    for n in (1, 2, 3):
        greet(peer4(n, oc))

    own = pl.ds(pl.multiple_of(c * 256, 256), 256)
    others = pl.ds(pl.multiple_of(oc * 256, 256), 256)

    top, bottom = slice(0, 256), slice(256, 512)

    def g_copy(i):
        owner, rows, n = (
            (y, top, 1), (y, bottom, 3), (y, bottom, 1), (y, top, 3),
            ((y + 3) % 4, top, 1), ((y + 1) % 4, bottom, 3),
        )[i]
        part = gbuf.at[owner, rows]
        return remote(part, part, g_ss.at[i], g_rs.at[i], (seq, (y + n) % 4))

    def wa_copy(n):
        return remote(wown.at[:, own], wst.at[c, zq, a3, a2, c], wa_ss.at[n - 1], wa_rs.at[n - 1], peer4(n))

    def wb_copy(n):
        return remote(wown.at[:, others], wst.at[oc, zq, a2, a3, c], wb_ss.at[n - 1], wb_rs.at[n - 1], peer4(n, oc))

    w0 = remote(wown.at[:, others], wst.at[oc, zq, a2, a3, c], w0_ss, w0_rs, other)

    def scan_piece1(i, n):
        to = (m + n) % 16
        return remote(sb.at[i, to], s1.at[i, m], p1_ss.at[i, n - 1], p1_rs.at[i, n - 1], (group * 16 + to, y))

    def scan_piece2(i, n):
        return remote(s2s.at[i], s2.at[i, group], p2_ss.at[i, n - 1], p2_rs.at[i, n - 1], (((group + n) % 8) * 16 + m, y))

    def scan_piece3(i, n):
        to = (m + n) % 16
        return remote(s3s.at[i, to], state.at[i, m], p3_ss.at[i, n - 1], p3_rs.at[i, n - 1], (group * 16 + to, y))

    def scan_own(i, product):
        def one(h, cols):
            s = product(cols).astype(BF16)
            sb[i, h * 4 : h * 4 + 4] = s.reshape(4, 32, D)

        each_head(one)
        s1[i, m] = sb[i, m]

    def scan_start(i):
        times(1, 16, lambda n: scan_piece1(i, n).start())

    def scan_total(i):
        times(1, 16, lambda n: scan_piece1(i, n).wait_recv())
        total = s1[i, 0].astype(F32)
        for j in range(1, 16):
            total += s1[i, j].astype(F32)
        s2s[i] = total.astype(s2s.dtype)
        times(1, 8, lambda n: scan_piece2(i, n).start())
        s2[i, group] = jnp.zeros_like(s2[i, group])

    def scan_back(i):
        times(1, 8, lambda n: scan_piece2(i, n).wait_recv())
        run = jnp.zeros((32, D), F32)
        for j in range(8):
            counts = (j < group) if i == 0 else (j > group)
            run += jnp.where(counts, s2[i, j].astype(F32), 0.0)
        for j in range(16) if i == 0 else range(15, -1, -1):
            s3s[i, j] = run.astype(BF16)
            run += s1[i, j].astype(F32)
        times(1, 16, lambda n: scan_piece3(i, n).start())
        state[i, m] = s3s[i, m]

    def scan_get(i):
        times(1, 16, lambda n: scan_piece3(i, n).wait_recv())

    def state_of(i, h):
        return state[i, pl.ds(h * 4, 4)].reshape(D, D)

    loads[0].wait()
    loads[1].wait()
    scan_own(0, lambda cols: dot_tn(k[:, cols], v[:, cols]))
    loads[2].wait()
    wst[c, zq, a3, a2, c] = wown[:, own]

    pl.semaphore_wait(barrier, 30)

    scan_start(0)
    for n in (2, 1, 3):
        wa_copy(n).start()
        wb_copy(n).start()
    w0.start()
    loads[4].wait()
    for i in range(4):
        g_copy(i).start()
    loads[3].wait()

    def lower(n, height):
        row = lax.broadcasted_iota(jnp.int32, (D, n), 0) + height
        col = lax.broadcasted_iota(jnp.int32, (D, n), 1)
        return row >= col

    def upper(n):
        row = lax.broadcasted_iota(jnp.int32, (D, n), 0)
        col = lax.broadcasted_iota(jnp.int32, (D, n), 1)
        return col >= row

    def attend(h, cols):
        for r in range(4):
            n = (r + 1) * D
            rows = slice(r * D, n)
            s = dot_nt(q[rows, cols], k[:n, cols])
            s = jnp.where(lower(n, r * D), s, 0.0).astype(BF16)
            av[rows, cols] = dot_nn(s, v[:n, cols])

    heads(attend)

    scan_total(0)

    for i in range(2):
        g_copy(i).wait_recv()
        g_copy(i + 4).start()

    def w2_copy(n, zs):
        part = wst.at[c, zs, a3, a2]
        return remote(part, part, w2_ss.at[n - 1], w2_rs.at[n - 1], peer2(n))

    def w3_copy(d, n, zs):
        part = wst.at[c, zs, a3, (a2 + d) % 4]
        return remote(part, part, w3_ss.at[d, n - 1], w3_rs.at[d, n - 1], peer3(n))

    def w4_copy(d, e):
        part = wst.at[c, :, (a3 + e) % 4, (a2 + d) % 4]
        return remote(part, part, w4_ss.at[d, e], w4_rs.at[d, e], other)

    def w3_start(d):
        for n, zs in hops:
            w3_copy(d, n, zs).start()
        w4_copy(d, 0).start()

    w0.wait_recv()
    for n in (1, 3, 2):
        wa_copy(n).wait_recv()
        wb_copy(n).wait_recv()
    for n, zs in hops:
        w2_copy(n, zs).start()
    w3_start(0)
    qt[...] = q[...].T
    gt[y] = gbuf[y].T
    for n, zs in hops:
        w2_copy(n, zs).wait_recv()
        if n != 2:
            w3_start(4 - n or 2)

    def attend_t(h, cols):
        for r in range(4):
            rows = slice(r * D, (r + 1) * D)
            s = dot_nt(k[rows, cols], q[r * D :, cols])
            at[h, rows, r * D :] = jnp.where(upper(T - r * D), s, 0.0).astype(BF16)

    scan_back(0)
    heads(attend_t)

    for i in range(2, 6):
        g_copy(i).wait_recv()
    for n in (1, 3, 2):
        gt[(y + n) % 4] = gbuf[(y + n) % 4].T

    scan_get(0)

    def rec(h, cols):
        outb[:, cols] = (SCALE * (av[:, cols] + dot_nn(q[:, cols], state_of(0, h)))).astype(BF16)

    each_head(rec)

    def r1_copy(i):
        return remote(rs.at[i], r1.at[i], r1_ss.at[i], r1_rs.at[i], other)

    def contribute(i):
        mine = dot_nn(gt[i], outb[:, own])
        theirs = dot_nn(gt[i], outb[:, others])
        for zi in range(4):
            for xi in range(4):
                rows = slice((zi * 4 + xi) * 32, (zi * 4 + xi) * 32 + 32)
                of_x, of_z = oc * xi + c * zi, oc * zi + c * xi
                hf[i, of_x, of_z] = mine[rows].reshape(2, 16, 256)
                rs[i, of_z, of_x] = theirs[rows].reshape(2, 16, 256).astype(BF16)
        r1_copy(i).start()

    for i, d in enumerate((0, 3, 1, 2)):
        contribute(i)
        for n, zs in hops:
            w3_copy(d, n, zs).wait_recv()
            if n != 2:
                w4_copy(d, 4 - n or 2).start()

    def r2_copy(p, d, n):
        to = peer3(4 if n == 2 and p == 1 else n)
        part = (a2 + d) % 4
        zs = slice(2 * p, 2 * p + 2)
        return remote(
            hb.at[n - 1, part, zs], r2.at[n - 1, part, zs], r2_ss.at[p, d, n - 1], r2_rs.at[p, d, n - 1], to
        )

    def pair(p):
        for i in (2 * p, 2 * p + 1):
            r1_copy(i).wait_recv()
            for n in (1, 3, 2):
                u = (a3 + n) % 4
                hb[n - 1, :, i] = (hf[i, u] + r1[i, u].astype(F32)).astype(BF16)
            h2[:, i] = hf[i, a3] + r1[i, a3].astype(F32)
        for d in (1, 3, 2, 0):
            for n in (1, 3, 2):
                r2_copy(p, d, n).start()

    pair(0)

    def project(half, cols):
        first = 1 - half
        total = None
        for i in range(4):
            w = [
                wst[half, i, first * xi + half * zi, first * zi + half * xi].reshape(32, 256)
                for zi in range(4)
                for xi in range(4)
            ]
            part = dot_nn(gbuf[i], jnp.concatenate(w, axis=0))
            total = part if total is None else total + part
        ag[:, cols] = total.astype(BF16)

    project(c, own)
    for d in range(4):
        for e in range(4):
            w4_copy(d, e).wait_recv()
    project(oc, others)

    scan_own(1, lambda cols: dot_nn(qt[cols], ag[:, cols]))
    scan_start(1)

    pair(1)

    def back(h, cols):
        for r in range(4):
            n = (r + 1) * D
            rows = slice(r * D, n)
            s = dot_nt(ag[rows, cols], v[:n, cols])
            s = jnp.where(lower(n, r * D), s, 0.0).astype(BF16)
            total = dot_nn(s, k[:n, cols]) + dot_nt(ag[rows, cols], state_of(0, h))
            outb[rows, cols] = (SCALE * total).astype(BF16)

    def back_kv(h, cols):
        for r in range(4):
            rows = slice(r * D, (r + 1) * D)
            mask = upper(T - r * D)
            s = dot_nt(v[rows, cols], ag[r * D :, cols])
            s = jnp.where(mask, s, 0.0).astype(BF16)
            kpart[rows, cols] = dot_nn(s, q[r * D :, cols])
            vpart[rows, cols] = dot_nn(at[h, rows, r * D :], ag[r * D :, cols])

    heads(back)
    q_store = pltpu.make_async_copy(outb, q_out, store_sem.at[0])
    q_store.start()
    scan_total(1)

    def r3_copy(n, zs):
        slot = (n if n < 4 else 2) - 1
        return remote(h2b.at[slot, zs], r3.at[slot, zs], r3_ss.at[n - 1], r3_rs.at[n - 1], peer2(n))

    for d in (1, 3, 2, 0):
        part = (a2 + d) % 4
        total = h2[part]
        for n in (1, 3, 2):
            for p in range(2):
                r2_copy(p, d, n).wait_recv()
            total += r2[n - 1, part].astype(F32)
        if d:
            h2b[d - 1] = total.astype(BF16)
            for n, zs in hops:
                if n == d or n == d + 2 == 4:
                    r3_copy(n, zs).start()
        else:
            h2[part] = total

    def ra_copy(n):
        return remote(h3.at[(zq + n) % 4, c], ra.at[n - 1], ra_ss.at[n - 1], ra_rs.at[n - 1], peer4(n))

    def rb_copy(n):
        return remote(h3.at[(zq + n) % 4, oc], rb.at[n], rb_ss.at[n], rb_rs.at[n], peer4(n, oc) if n else other)

    heads(back_kv)

    for n, zs in hops:
        r3_copy(n, zs).wait_recv()
    for i in range(4):
        total = h2[a2, i]
        for n in range(3):
            total += r3[n, i].astype(F32)
        h3[i] = total
    for n in (2, 1, 3):
        ra_copy(n).start()
        rb_copy(n).start()
    rb_copy(0).start()

    scan_back(1)

    scan_get(1)

    q_store.wait()

    def final_k(h, cols):
        outb[:, cols] = (SCALE * (kpart[:, cols] + dot_nt(v[:, cols], state_of(1, h)))).astype(BF16)

    def final_v(h, cols):
        ag[:, cols] = (SCALE * (vpart[:, cols] + dot_nn(k[:, cols], state_of(1, h)))).astype(BF16)

    k_store = pltpu.make_async_copy(outb, k_out, store_sem.at[1])
    v_store = pltpu.make_async_copy(ag, v_out, store_sem.at[2])
    each_head(final_k)
    k_store.start()
    each_head(final_v)
    v_store.start()

    mine = h3[zq, c]
    for n in range(3):
        ra_copy(n + 1).wait_recv()
        mine += ra[n]
    wo[:, own] = mine * WSCALE
    rb_copy(0).wait_recv()
    theirs = rb[0]
    for n in range(1, 4):
        rb_copy(n).wait_recv()
        theirs += rb[n]
    wo[:, others] = theirs * WSCALE
    w_store = pltpu.make_async_copy(wo, w_out, store_sem.at[3])
    w_store.start()

    w0.wait_send()
    for n, zs in hops:
        w2_copy(n, zs).wait_send()
        r3_copy(n, zs).wait_send()
        for d in range(4):
            w3_copy(d, n, zs).wait_send()
    for n in (1, 2, 3):
        wa_copy(n).wait_send()
        wb_copy(n).wait_send()
        ra_copy(n).wait_send()
    for n in range(4):
        rb_copy(n).wait_send()
        r1_copy(n).wait_send()
        for d in range(4):
            w4_copy(d, n).wait_send()
    for p in range(2):
        for d in range(4):
            for n in (1, 2, 3):
                r2_copy(p, d, n).wait_send()
    for i in range(6):
        g_copy(i).wait_send()
    for i in range(2):
        times(1, 16, lambda n, i=i: scan_piece1(i, n).wait_send())
        times(1, 8, lambda n, i=i: scan_piece2(i, n).wait_send())
        times(1, 16, lambda n, i=i: scan_piece3(i, n).wait_send())
    k_store.wait()
    v_store.wait()
    w_store.wait()


def hand_over(*refs):
    ins, outs, held, sem = refs[:4], refs[4:8], refs[8:12], refs[12]
    reads = [pltpu.make_async_copy(ins[i], held[i], sem.at[0, i]) for i in range(4)]
    writes = [pltpu.make_async_copy(held[i], outs[i], sem.at[1, i]) for i in range(4)]
    for read in reads:
        read.start()
    for read, write in zip(reads, writes):
        read.wait()
        write.start()
    for write in writes:
        write.wait()


def per_device(queries, keys, values, grad_out, out_weight):
    def vmem(*shape, dtype=BF16):
        return pltpu.VMEM(shape, dtype)

    def sems(*shape):
        return [pltpu.SemaphoreType.DMA(shape)] * 2

    wide = (T, T)
    scratch = [
        vmem(*wide), vmem(*wide), vmem(*wide),
        vmem(4, *wide), vmem(4, *wide), vmem(*wide),
        vmem(16, 512),
        vmem(2, 4, 4, 4, 2, 16, 256),
        vmem(*wide, dtype=F32),
        vmem(4, *wide),
        vmem(*wide),
        vmem(*wide),
        vmem(*wide, dtype=F32), vmem(*wide, dtype=F32),
        vmem(2, 16, 32, D), vmem(2, 16, 32, D),
        vmem(2, 32, D), vmem(2, 8, 32, D),
        vmem(2, 16, 32, D), vmem(2, 16, 32, D),
        vmem(4, 4, 4, 2, 16, 256, dtype=F32),
        vmem(4, 4, 4, 2, 16, 256),
        vmem(4, 4, 4, 2, 16, 256),
        vmem(3, 4, 4, 2, 16, 256),
        vmem(3, 4, 4, 2, 16, 256),
        vmem(4, 4, 2, 16, 256, dtype=F32),
        vmem(3, 4, 2, 16, 256),
        vmem(3, 4, 2, 16, 256),
        vmem(4, 2, 16, 256, dtype=F32),
        vmem(3, 16, 256, dtype=F32),
        vmem(4, 16, 256, dtype=F32),
        vmem(16, 512, dtype=F32),
        pltpu.SemaphoreType.DMA((5,)), pltpu.SemaphoreType.DMA((4,)),
        *sems(6),
        pltpu.SemaphoreType.DMA, pltpu.SemaphoreType.DMA,
        *sems(3), *sems(3), *sems(4), *sems(4, 4), *sems(4, 4),
        *sems(2, 15), *sems(2, 7), *sems(2, 15),
        *sems(4), *sems(2, 4, 3), *sems(4), *sems(3), *sems(4),
    ]
    shape = jax.ShapeDtypeStruct(wide, BF16)
    outs = pl.pallas_call(
        kernel,
        out_shape=(shape, shape, shape, jax.ShapeDtypeStruct((16, 512), F32)),
        in_specs=[pl.BlockSpec(memory_space=pl.ANY)] * 5,
        out_specs=[pl.BlockSpec(memory_space=pl.ANY)] * 4,
        scratch_shapes=scratch,
        compiler_params=pltpu.CompilerParams(
            collective_id=0, has_side_effects=True, vmem_limit_bytes=56 * 2**20
        ),
        name="attention_backward",
    )(queries, keys, values, grad_out, out_weight)
    return pl.pallas_call(
        hand_over,
        out_shape=tuple(jax.ShapeDtypeStruct(a.shape, a.dtype) for a in outs),
        in_specs=[pl.BlockSpec(memory_space=pl.ANY)] * 4,
        out_specs=[pl.BlockSpec(memory_space=pl.ANY)] * 4,
        scratch_shapes=[vmem(*a.shape, dtype=a.dtype) for a in outs] + [pltpu.SemaphoreType.DMA((2, 4))],
        name="hand_over",
    )(*outs)


def solution(mesh):
    spec = P("seq", "head")
    return jax.shard_map(
        per_device, mesh=mesh, in_specs=(spec,) * 5, out_specs=(spec,) * 4, check_vma=False
    )
```
